32 devices in a mesh: rows: 4 (over x, core), cols: 8 (over z, y).
Axes of the slice: x: 2, y: 2, z: 4, core: 2. Of those that a mesh axis runs over, the one named last changes fastest.
Arguments:
- video: bfloat16 [1920, 128, 128], P('cols', 'rows'), may hold values from -8 to 8, as said below
- fore_prev: float32 [1920, 128, 128], P('cols', 'rows'), may hold values from -4 to 4
- mult: float32 [1920, 128, 128], P('cols', 'rows'), may hold values from -4 to 4
- dual_tv: float32 [3, 1920, 128, 128], P(None, 'cols', 'rows'), may hold values from -1 to 1
- shrink: float32 [2], replicated, may hold values from 0.3 to 3
- tv_weight: float32 [2], replicated, may hold values from 0.3 to 1.5
Outputs:
- low_rank: float32 [1920, 128, 128], P('cols', 'rows')
- fore: float32 [1920, 128, 128], P('cols', 'rows')
- mult_out: float32 [1920, 128, 128], P('cols', 'rows')
- dual_out: float32 [3, 1920, 128, 128], P(None, 'cols', 'rows')
The draws below stay inside these ranges and needn't reach their ends.
Inputs may be any that keep to these rules, and one draw needn't show every extreme that they name: `video`: pixel values.
All inputs are finite; a program needn't handle non-finite values.
Results may differ from the reference program's by a relative error of at most 0.0003.
Values sent between devices are 32-bit elements; how exact they have to be, the bound alone decides.
A program may use at most 128 MiB of HBM per device.

```python
import math
import jax
import jax.numpy as jnp
from jax import lax

CAMS = 2
F = 64
WIDTH = 1920
TV_STEPS = 4
H = 128


def draw_video(key, part):
    keys = jax.random.split(key, 3)
    comps = 6
    coef = jax.random.normal(keys[0], (CAMS, comps, F), jnp.float32)
    spatial = jax.random.normal(keys[1], (CAMS, comps, H, WIDTH), jnp.float32)
    colpos = jnp.arange(WIDTH, dtype=jnp.float32) / WIDTH
    rowpos = jnp.arange(H, dtype=jnp.float32) / H
    noise = 0.5 * jax.random.normal(keys[2], (CAMS, F, H, WIDTH), jnp.float32)
    total = jnp.zeros((CAMS, F, H, WIDTH), jnp.float32)
    for index in range(comps):
        across = colpos if index % 2 == 0 else 1.0 - colpos
        downward = rowpos if index % 3 == 0 else 1.0 - rowpos
        envelope = 10.0 ** (across[None, :] + 0.5 * downward[:, None] - 0.9)
        total = total + coef[:, index, :, None, None] * (spatial[:, index] * envelope[None])[:, None]
    result = jnp.clip(0.45 * total + noise, -8.0, 8.0)
    result = jnp.transpose(result, (3, 2, 0, 1)).reshape(WIDTH, H, CAMS * F)
    return result.astype(jnp.bfloat16)


def block_levels(rng, extent, pieces, least, top_value):
    level, own = 1.0, jax.random.fold_in(rng, 6)
    for axis_at, blocks in pieces:
        draws = jnp.exp(jax.random.uniform(jax.random.fold_in(own, axis_at), (blocks,), jnp.float32, least / len(pieces), top_value / len(pieces)))
        level = level * jnp.repeat(draws, extent[axis_at] // blocks).reshape([-1 if axis == axis_at else 1 for axis in range(len(extent))])
    return level


def normal_values(rng, shape, scale, reach, shards=(), kind=jnp.bfloat16):
    loudness = block_levels(rng, shape, shards, -0.22, 0.18) if shards else 1.0
    drawn = jax.random.normal(rng, shape, jnp.float32) * scale * loudness
    return jnp.minimum(jnp.maximum(drawn, -reach), reach).astype(kind)


def setup_inputs(seed: int = 0) -> dict:
    streams_of = jax.random.split(jax.random.key(seed), 7)
    return {
        "video": draw_video(jax.random.fold_in(streams_of[6], 71), 0),
        "fore_prev": normal_values(streams_of[1], (WIDTH, H, CAMS * F), 0.5, 4.0, ((0, 8), (1, 4)), jnp.float32),
        "mult": normal_values(streams_of[2], (WIDTH, H, CAMS * F), 0.5, 4.0, ((0, 8), (1, 4)), jnp.float32),
        "dual_tv": jnp.clip(jax.random.uniform(streams_of[3], (3, WIDTH, H, CAMS * F), jnp.float32, -1.0, 1.0) * block_levels(streams_of[3], (3, WIDTH, H, CAMS * F), ((1, 8), (2, 4)), -0.4, 0.0), -1.0, 1.0),
        "shrink": jnp.clip(jnp.exp(jax.random.uniform(streams_of[4], (CAMS,), jnp.float32, math.log(0.3), math.log(3.0))), 0.3, 3.0),
        "tv_weight": jnp.clip(jnp.exp(jax.random.uniform(streams_of[5], (CAMS,), jnp.float32, math.log(0.3), math.log(1.5))), 0.3, 1.5),
    }


MU = 1.25
KAPPA = 0.08

def prev_local(field, axis):
    count = field.shape[axis]
    zeros = jnp.zeros_like(lax.slice_in_dim(field, 0, 1, axis=axis))
    return jnp.concatenate([zeros, lax.slice_in_dim(field, 0, count - 1, axis=axis)], axis)

def next_local(field, axis):
    count = field.shape[axis]
    zeros = jnp.zeros_like(lax.slice_in_dim(field, 0, 1, axis=axis))
    return jnp.concatenate([lax.slice_in_dim(field, 1, count, axis=axis), zeros], axis)

def shrink_filter(gram, shrink):
    frames = gram.shape[-1]
    trace = jnp.trace(gram, axis1=1, axis2=2)
    tau = shrink * trace / frames
    shifted = gram + tau[:, None, None] * jnp.eye(frames, dtype=gram.dtype)[None]
    factor = jnp.linalg.cholesky(shifted)
    return jax.vmap(lambda lower, right: jax.scipy.linalg.cho_solve((lower, True), right))(factor, gram)

def divergence(p_f, p_h, p_w, masks):
    mask_f, mask_h, mask_w = masks
    q_f = p_f * mask_f
    q_h = p_h * mask_h
    q_w = p_w * mask_w
    return q_f - prev_local(q_f, 2) + (q_h - prev_local(q_h, 1)) + (q_w - prev_local(q_w, 0))

def gradient(field, masks):
    mask_f, mask_h, mask_w = masks
    return ((next_local(field, 2) - field) * mask_f, (next_local(field, 1) - field) * mask_h, (next_local(field, 0) - field) * mask_w)

def reference(video, fore_prev, mult, dual_tv, shrink, tv_weight):
    frames = video.astype(jnp.float32)
    data = frames - fore_prev + mult / MU
    count_w, count_h, merged = data.shape
    cams = shrink.shape[0]
    count_f = merged // cams
    flat = data.reshape(count_w * count_h, cams, count_f)
    gram = jnp.einsum('pcf,pcg->cfg', flat, flat, precision=lax.Precision.HIGHEST)
    filt = shrink_filter(gram, shrink)
    low_rank = jnp.einsum('pcg,cgf->pcf', flat, filt, precision=lax.Precision.HIGHEST).reshape(count_w, count_h, merged)
    target = frames - low_rank + mult / MU
    mask_f = (jnp.arange(merged) % count_f < count_f - 1).astype(jnp.float32)[None, None, :]
    mask_h = (jnp.arange(count_h) < count_h - 1).astype(jnp.float32)[None, :, None]
    mask_w = (jnp.arange(count_w) < count_w - 1).astype(jnp.float32)[:, None, None]
    masks = (mask_f, mask_h, mask_w)
    lam = jnp.repeat(tv_weight, count_f)[None, None, :]
    p_f, p_h, p_w = (dual_tv[0], dual_tv[1], dual_tv[2])
    for step in range(TV_STEPS):
        field = target - lam * divergence(p_f, p_h, p_w, masks)
        g_f, g_h, g_w = gradient(field, masks)
        p_f = jnp.clip(p_f + KAPPA / lam * g_f, -1.0, 1.0)
        p_h = jnp.clip(p_h + KAPPA / lam * g_h, -1.0, 1.0)
        p_w = jnp.clip(p_w + KAPPA / lam * g_w, -1.0, 1.0)
    fore = target - lam * divergence(p_f, p_h, p_w, masks)
    mult_out = mult + MU * (frames - low_rank - fore)
    return (low_rank, fore, mult_out, jnp.stack([p_f, p_h, p_w]))
```

```python
import functools
import jax
import jax.numpy as jnp
from jax import lax
from jax.experimental import pallas as pl
from jax.experimental.pallas import tpu as pltpu
from jax.sharding import PartitionSpec as P

TV_STEPS = 4
MU = 1.25
KAPPA = 0.08
MESH = pl.DeviceIdType.MESH
F32 = jnp.float32
BF16 = jnp.bfloat16


def split(x):
    hi = x.astype(BF16)
    return hi, (x - hi.astype(F32)).astype(BF16)


def dot(a, b, dims):
    return lax.dot_general(a, b, (dims, ((), ())), preferred_element_type=F32)


def pick(count, most):
    return max(d for d in range(1, most + 1) if count % d == 0)


def stages_of(rows, cols):
    stages = []
    for axis, size in (("rows", rows), ("cols", cols)):
        low = 1
        while low < size:
            high = min(low * 4, size)
            stages.append((axis, [m * low for m in range(1, high // low)]))
            low = high
    return stages


def kernel(dims, video, fore_prev, mult, dual, shrink, weight,
           low, mout, p, u, ha_out, wl_out,
           vid, sh, su, ha, ub, sw, suc, wl, uc, sdh, sdw, dh, dw,
           gacc, gin, mat, wide, in_sem, p_sem, g_send, g_recv, r_send, r_recv, c_send, c_recv):
    rows, cols, W, R = dims
    T = R // 8
    my_r, my_c = lax.axis_index("rows"), lax.axis_index("cols")
    stages = stages_of(rows, cols)

    n_in = pick(W, 10)
    wi = W // n_in
    ins = ((video, vid), (fore_prev, low), (mult, mout))

    def in_copy(j, k):
        src, dst = ins[j]
        at = pl.ds(k * wi, wi)
        return pltpu.make_async_copy(src.at[at], dst.at[at], in_sem.at[j, k])

    def p_copy(j):
        return pltpu.make_async_copy(dual.at[j], p.at[j], p_sem.at[j])

    def start_in(k, _):
        for j in range(3):
            in_copy(j, k).start()
        return 0

    lax.fori_loop(0, n_in, start_in, 0)
    for j in range(3):
        p_copy(j).start()

    def partner(axis, mask):
        return (my_r ^ mask, my_c) if axis == "rows" else (my_r, my_c ^ mask)

    above = (lax.rem(my_r + rows - 1, rows), my_c)
    below = (lax.rem(my_r + 1, rows), my_c)
    left = (my_r, lax.rem(my_c + cols - 1, cols))
    right = (my_r, lax.rem(my_c + 1, cols))
    upright = (above[0], right[1])
    downleft = (below[0], left[1])
    has_above, has_below = my_r > 0, my_r < rows - 1
    has_left, has_right = my_c > 0, my_c < cols - 1
    barrier = pltpu.get_barrier_semaphore()
    greet = [partner(a, m) for a, ms in stages for m in ms]
    greet += [above, below, left, right, upright, downleft]
    for other in greet:
        pl.semaphore_signal(barrier, inc=1, device_id=other, device_id_type=MESH)

    sub = lax.broadcasted_iota(jnp.int32, (8, 128), 0)
    lane = lax.broadcasted_iota(jnp.int32, (8, 128), 1)
    first_cam = lane < 64
    lam = jnp.where(first_cam, weight[0], weight[1])
    lam1 = lam[0:1]
    top, bottom = sub == 0, sub == 7
    mf = jnp.where((lane % 64) < 63, 1.0, 0.0).astype(F32)
    step_c = jnp.where(first_cam, KAPPA / weight[0], KAPPA / weight[1])
    cf = step_c * mf
    mh = jnp.where(bottom & jnp.logical_not(has_below), 0.0, 1.0).astype(F32)
    ch_last = step_c * mh

    def zero_rows(ref, count):
        def body(i, _):
            for s in range(count):
                ref[s, i] = jnp.zeros((1, 128), F32)
            return 0
        lax.fori_loop(0, W, body, 0)

    @pl.when(jnp.logical_not(has_above))
    def _():
        zero_rows(ha, TV_STEPS + 1)

    @pl.when(jnp.logical_not(has_below))
    def _():
        zero_rows(ub, TV_STEPS)

    @pl.when(jnp.logical_not(has_left))
    def _():
        wl[...] = jnp.zeros_like(wl)

    @pl.when(jnp.logical_not(has_right & has_above))
    def _():
        dh[...] = jnp.zeros_like(dh)

    @pl.when(jnp.logical_not(has_left & has_below))
    def _():
        dw[...] = jnp.zeros_like(dw)

    wide[...] = jnp.zeros_like(wide)
    gu = pick(wi, 8)

    def gram_chunk(k, _):
        for j in range(3):
            in_copy(j, k).wait()

        def body(i, _):
            at = pl.ds(k * wi + i * gu, gu)
            base = vid[at].astype(F32) + mout[at] * (1.0 / MU)
            data = base - low[at]
            mout[at] = base
            low[at] = data
            hi, lo = split(data.reshape(gu * R, 128))
            wide[...] += dot(hi, jnp.concatenate([hi, lo], 1), ((0,), (0,)))
            return 0

        return lax.fori_loop(0, wi // gu, body, 0)

    lax.fori_loop(0, n_in, gram_chunk, 0)
    cross = wide[:, 128:]
    full = wide[:, :128] + cross + cross.T
    half = lax.broadcasted_iota(jnp.int32, (64, 128), 1) < 64
    gacc[0] = jnp.where(half, full[:64], full[64:])

    pl.semaphore_wait(barrier, len(greet))
    slot = 0
    sends = []
    for i, (axis, masks) in enumerate(stages):
        copies = []
        for m in masks:
            copies.append(pltpu.make_async_remote_copy(
                src_ref=gacc.at[i], dst_ref=gin.at[slot], send_sem=g_send.at[slot],
                recv_sem=g_recv.at[slot], device_id=partner(axis, m), device_id_type=MESH))
            copies[-1].start()
            slot += 1
        total = gacc[i]
        for j, c in enumerate(copies):
            c.wait_recv()
            total = total + gin[slot - len(masks) + j]
        gacc[i + 1] = total
        sends += copies
    for c in sends:
        c.wait_send()

    gram = gacc[len(stages)]
    ri = lax.broadcasted_iota(jnp.int32, (64, 128), 0)
    ci = lax.broadcasted_iota(jnp.int32, (64, 128), 1)
    eye = ri == (ci % 64)
    diag = jnp.where(eye, gram, 0.0)
    tr0 = jnp.sum(jnp.where(half, diag, 0.0))
    tr1 = jnp.sum(jnp.where(half, 0.0, diag))
    tau = jnp.where(half, shrink[0] * tr0 / 64.0, shrink[1] * tr1 / 64.0)
    a0 = gram + jnp.where(eye, tau, 0.0)
    mat[...] = a0
    tail = (ci % 64) == 63

    def pivot(k, a):
        r = mat[pl.ds(k, 1), :]
        d = jnp.where(half[:1], r[:, 0:1], r[:, 64:65])
        c = jnp.where(half, a[:, 0:1], a[:, 64:65])
        inv = 1.0 / d
        rd = r * inv
        here = ri == k
        new = jnp.where(here, rd, a - c * rd)
        col = jnp.where(here, inv, -c * inv)
        out = jnp.where(tail, col, pltpu.roll(new, 127, 1))
        mat[...] = out
        return out

    inverse = lax.fori_loop(0, 64, pivot, a0)
    filt = jnp.where(eye, 1.0, 0.0) - tau * inverse
    filt = jnp.concatenate([jnp.where(half, filt, 0.0), jnp.where(half, 0.0, filt)], 0)
    fhi, flo = split(filt)

    n_unroll = pick(W, 8)
    n_iter = W // n_unroll
    nch = pick(n_iter, 3)
    per = n_iter // nch
    span = per * n_unroll

    def remote(src, dst, send, recv, to):
        return pltpu.make_async_remote_copy(src_ref=src, dst_ref=dst, send_sem=send,
                                            recv_sem=recv, device_id=to, device_id_type=MESH)

    def row_h(s, k):
        at = pl.ds(k * span, span)
        return remote(sh.at[s, at], ha.at[s, at], r_send.at[0, s, k], r_recv.at[0, s, k], below)

    def row_u(s, k):
        at = pl.ds(k * span, span)
        return remote(su.at[s, at], ub.at[s, at], r_send.at[1, s, k], r_recv.at[1, s, k], above)

    def col_w(s):
        return remote(sw.at[s], wl.at[s], c_send.at[0, s], c_recv.at[0, s], right)

    def col_u(s):
        return remote(suc.at[s], uc.at[s], c_send.at[1, s], c_recv.at[1, s], left)

    def dia_h(s):
        return remote(sdh.at[s], dh.at[s], c_send.at[2, s], c_recv.at[2, s], downleft)

    def dia_w(s):
        return remote(sdw.at[s], dw.at[s], c_send.at[3, s], c_recv.at[3, s], upright)

    def send_rows(s, k, last):
        @pl.when(has_below)
        def _():
            row_h(s, k).start()
        if not last:
            @pl.when(has_above)
            def _():
                row_u(s, k).start()

    def send_first(s, last):
        if last:
            return

        @pl.when(has_left)
        def _():
            suc[s] = u[0]
            col_u(s).start()

        @pl.when(has_left & has_below)
        def _():
            sdh[s] = p[1, 0, R - 1:R, :]
            dia_h(s).start()

    def send_end(s, last):
        @pl.when(has_right)
        def _():
            sw[s] = p[2, W - 1]
            col_w(s).start()
        if not last:
            @pl.when(has_right & has_above)
            def _():
                sdw[s] = p[2, W - 1, 0:1, :]
                dia_w(s).start()

    def tiles(ref, *at):
        return [ref[(*at, pl.ds(8 * t, 8))] for t in range(T)]

    def new_field(s, w, target, pf, ph, pw, before):
        qh = ph[:-1] + [ph[-1] * mh]
        rolled = [pltpu.roll(x, 1, 0) for x in qh]
        out = []
        for t in range(T):
            qf = pf[t] * mf
            prev = jnp.where(top, rolled[t - 1] if t else 0.0, rolled[t])
            div = (qf - pltpu.roll(qf, 1, 1)) + (qh[t] - prev) + (pw[t] - before[t])
            out.append(target[t] - lam * div)
        for t in range(T):
            u[w, pl.ds(8 * t, 8)] = out[t]
        sh[s, w] = ph[-1][7:8]
        su[s, w] = out[0][0:1]

    def finish_field(s):
        @pl.when(jnp.logical_not(has_right))
        def _():
            for t in range(T):
                at = pl.ds(8 * t, 8)
                u[W - 1, at] = u[W - 1, at] + lam * p[2, W - 1, at]
            su[s, W - 1] = su[s, W - 1] + lam1 * p[2, W - 1, 0:1]

    for j in range(3):
        p_copy(j).wait()

    def low_body(i, before):
        w0 = i * n_unroll
        at = pl.ds(w0, n_unroll)
        data = low[at].reshape(n_unroll * R, 128)
        hi, lo = split(data)
        lr = dot(hi, fhi, ((1,), (0,))) + (dot(lo, fhi, ((1,), (0,))) + dot(hi, flo, ((1,), (0,))))
        lr = lr.reshape(n_unroll, R, 128)
        low[at] = lr
        target_all = mout[at] - lr
        mout[at] = target_all
        for n in range(n_unroll):
            w = w0 + n
            pw = tiles(p, 2, w)
            target = [target_all[n, 8 * t:8 * t + 8] for t in range(T)]
            new_field(0, w, target, tiles(p, 0, w), tiles(p, 1, w), pw, before)
            before = pw
        return before

    zeros = [jnp.zeros((8, 128), F32)] * T
    before = zeros
    for k in range(nch):
        before = lax.fori_loop(k * per, (k + 1) * per, low_body, before)
        if k == nch - 1:
            finish_field(0)
        send_rows(0, k, False)
        if k == 0:
            send_first(0, False)
    send_end(0, False)

    def fixed(s, w):
        out = tiles(u, w)
        out[0] = out[0] + jnp.where(top, lam * ha[s, w], 0.0)
        return out

    def wait_h(s, k):
        @pl.when(has_above)
        def _():
            row_h(s, k).wait_recv()

    def wait_u(s, k):
        @pl.when(has_below)
        def _():
            row_u(s, k).wait_recv()

    def step(s, last):
        nxt = s + 1

        @pl.when(has_left)
        def _():
            col_w(s).wait_recv()

        @pl.when(has_left & has_below)
        def _():
            dia_w(s).wait_recv()

        @pl.when(has_right & has_above)
        def _():
            dia_h(s).wait_recv()

        @pl.when(has_right)
        def _():
            col_u(s).wait_recv()

        wait_h(s, 0)
        wait_u(s, 0)
        ub[s, 0] = ub[s, 0] + lam1 * dw[s]
        for t in range(T):
            at = pl.ds(8 * t, 8)
            u[0, at] = u[0, at] + lam * wl[s, at]

        def body(i, carry):
            now, before = carry
            w0 = i * n_unroll
            for n in range(n_unroll):
                w = w0 + n
                after = fixed(s, w + 1)
                pf, ph, pw = tiles(p, 0, w), tiles(p, 1, w), tiles(p, 2, w)
                under = ub[s, w] + lam1 * ph[-1][7:8]
                rolled = [pltpu.roll(x, 7, 0) for x in now]
                nf, nh, nw = [], [], []
                for t in range(T):
                    down = jnp.where(bottom, rolled[t + 1] if t < T - 1 else under, rolled[t])
                    ch = step_c if t < T - 1 else ch_last
                    nf.append(jnp.clip(pf[t] + cf * (pltpu.roll(now[t], 127, 1) - now[t]), -1.0, 1.0))
                    nh.append(jnp.clip(ph[t] + ch * (down - now[t]), -1.0, 1.0))
                    nw.append(jnp.clip(pw[t] + step_c * (after[t] - now[t]), -1.0, 1.0))
                for j, new in enumerate((nf, nh, nw)):
                    for t in range(T):
                        p[j, w, pl.ds(8 * t, 8)] = new[t]
                new_field(nxt, w, tiles(mout, w), nf, nh, nw, before)
                now, before = after, nw
            return now, before

        carry = (fixed(s, 0), zeros)
        for k in range(nch):
            if k:
                wait_u(s, k)
            if k + 1 < nch:
                wait_h(s, k + 1)
            else:
                @pl.when(has_right)
                def _():
                    ha[s, W] = dh[s]
                    for t in range(T):
                        at = pl.ds(8 * t, 8)
                        u[W, at] = uc[s, at] + lam * p[2, W - 1, at]

                @pl.when(jnp.logical_not(has_right))
                def _():
                    ha[s, W] = ha[s, W - 1]
                    u[W] = u[W - 1]
            carry = lax.fori_loop(k * per, (k + 1) * per, body, carry)
            if k == nch - 1:
                finish_field(nxt)
            send_rows(nxt, k, last)
            if k == 0:
                send_first(nxt, last)
        send_end(nxt, last)

    def step_body(s, _):
        step(s, False)
        return 0

    lax.fori_loop(0, TV_STEPS - 1, step_body, 0)
    step(TV_STEPS - 1, True)

    s = TV_STEPS

    @pl.when(has_left)
    def _():
        col_w(s).wait_recv()

    for k in range(nch):
        wait_h(s, k)

    wl_out[...] = wl[s]

    def halo_body(w, _):
        ha_out[w] = ha[s, w]
        return 0

    lax.fori_loop(0, W, halo_body, 0)

    def drain(s, last):
        @pl.when(has_below)
        def _():
            for k in range(nch):
                row_h(s, k).wait_send()

        @pl.when(has_right)
        def _():
            col_w(s).wait_send()

        if last:
            return

        @pl.when(has_above)
        def _():
            for k in range(nch):
                row_u(s, k).wait_send()

        @pl.when(has_left)
        def _():
            col_u(s).wait_send()

        @pl.when(has_left & has_below)
        def _():
            dia_h(s).wait_send()

        @pl.when(has_right & has_above)
        def _():
            dia_w(s).wait_send()

    def drain_body(s, _):
        drain(s, False)
        return 0

    lax.fori_loop(0, TV_STEPS, drain_body, 0)
    drain(TV_STEPS, True)


def export_kernel(dims, low, target, p, u, ha, wl, weight, low_o, fore_o, mout_o, p_o,
                  fore, mout, sem, f_sem, m_sem):
    W, R = dims
    T = R // 8
    whole = [pltpu.make_async_copy(p.at[j], p_o.at[j], sem.at[j]) for j in range(3)]
    whole.append(pltpu.make_async_copy(low, low_o, sem.at[3]))
    sub = lax.broadcasted_iota(jnp.int32, (8, 128), 0)
    lane = lax.broadcasted_iota(jnp.int32, (8, 128), 1)
    lam = jnp.where(lane < 64, weight[0], weight[1])
    unroll = pick(W, 8)
    iters = W // unroll
    nch = pick(iters, 3)
    per = iters // nch
    span = per * unroll
    for c in whole[:1]:
        c.start()

    def body(i, _):
        for n in range(unroll):
            w = i * unroll + n
            for t in range(T):
                at = pl.ds(8 * t, 8)
                f = u[w, at]
                if t == 0:
                    f = f + jnp.where(sub == 0, lam * ha[w], 0.0)
                fore[w, at] = f
                mout[w, at] = MU * (target[w, at] - f)
        return 0

    parts = []
    for k in range(nch):
        lax.fori_loop(k * per, (k + 1) * per, body, 0)
        if k == 0:
            for t in range(T):
                at = pl.ds(8 * t, 8)
                f = fore[0, at] + lam * wl[at]
                fore[0, at] = f
                mout[0, at] = MU * (target[0, at] - f)
        at = pl.ds(k * span, span)
        parts.append(pltpu.make_async_copy(fore.at[at], fore_o.at[at], f_sem.at[k]))
        parts.append(pltpu.make_async_copy(mout.at[at], mout_o.at[at], m_sem.at[k]))
        if k == 0:
            for c in whole[1:]:
                c.start()
        parts[-2].start()
        parts[-1].start()
    for c in whole + parts:
        c.wait()


def local(rows, cols, video, fore_prev, mult, dual_tv, shrink, tv_weight):
    W, R, L = video.shape
    S = TV_STEPS
    stages = stages_of(rows, cols)
    slots = sum(len(m) for _, m in stages)
    n_in = pick(W, 10)
    nch = pick(W // pick(W, 8), 3)
    vmem = lambda *shape: pltpu.VMEM(shape, F32)
    hbm = pl.BlockSpec(memory_space=pltpu.HBM)
    smem = pl.BlockSpec(memory_space=pltpu.SMEM)
    out = pl.BlockSpec(memory_space=pltpu.VMEM)
    dual = jax.ShapeDtypeStruct((3, W, R, L), F32)
    field = jax.ShapeDtypeStruct((W, R, L), F32)
    dma = pltpu.SemaphoreType.DMA
    low, target, p, u, ha, wl = pl.pallas_call(
        functools.partial(kernel, (rows, cols, W, R)),
        out_shape=(field, field, dual, jax.ShapeDtypeStruct((W + 1, R, L), F32),
                   jax.ShapeDtypeStruct((W, 1, L), F32), jax.ShapeDtypeStruct((R, L), F32)),
        in_specs=[hbm] * 4 + [smem] * 2,
        out_specs=(out,) * 6,
        scratch_shapes=[
            pltpu.VMEM((W, R, L), BF16),
            vmem(S + 1, W, 1, L), vmem(S + 1, W, 1, L),
            vmem(S + 1, W + 1, 1, L), vmem(S, W, 1, L),
            vmem(S + 1, R, L), vmem(S, R, L), vmem(S + 1, R, L), vmem(S, R, L),
            vmem(S, 1, L), vmem(S, 1, L), vmem(S, 1, L), vmem(S, 1, L),
            vmem(len(stages) + 1, 64, 128), vmem(slots, 64, 128),
            vmem(64, 128), vmem(128, 256),
            dma((3, n_in)), dma((3,)), dma((slots,)), dma((slots,)),
            dma((2, S + 1, nch)), dma((2, S + 1, nch)), dma((4, S + 1)), dma((4, S + 1)),
        ],
        compiler_params=pltpu.CompilerParams(
            collective_id=0, has_side_effects=True, vmem_limit_bytes=14 * 2**20),
        cost_estimate=pl.CostEstimate(flops=2 * 10**9, bytes_accessed=45 * 10**6, transcendentals=0),
        name="admm",
    )(video, fore_prev, mult, dual_tv, shrink, tv_weight)
    return pl.pallas_call(
        functools.partial(export_kernel, (W, R)),
        out_shape=(field, field, field, dual),
        in_specs=[out] * 6 + [smem],
        out_specs=(hbm,) * 4,
        scratch_shapes=[vmem(W, R, L), vmem(W, R, L), dma((4,)), dma((nch,)), dma((nch,))],
        compiler_params=pltpu.CompilerParams(vmem_limit_bytes=12 * 2**20),
        cost_estimate=pl.CostEstimate(flops=10**7, bytes_accessed=24 * 10**6, transcendentals=0),
        name="write_out",
    )(low, target, p, u, ha, wl, tv_weight)


def solution(mesh):
    spec = P("cols", "rows", None)
    dual = P(None, "cols", "rows", None)
    return jax.shard_map(
        functools.partial(local, mesh.shape["rows"], mesh.shape["cols"]),
        mesh=mesh,
        in_specs=(spec, spec, spec, dual, P(), P()),
        out_specs=(spec, spec, spec, dual),
        check_vma=False,
    )
```
